128 devices in a mesh: blk: 16 (over y, x_lo, core), split: 8 (over z, x_hi).
Axes of the slice: x: 4 (x_hi: 2, x_lo: 2; x = x_hi * 2 + x_lo), y: 4, z: 4, core: 2. Of those that a mesh axis runs over, the one named last changes fastest.
Arguments:
- points: bfloat16 [65536, 128], P(('blk', 'split')), may hold values from -4 to 4
- inv_length: float32 [128], replicated, may hold values from 0.2 to 1
- amplitude: float32 [], replicated, may hold values from 0.1 to 0.4
- noise: float32 [65536], P(('blk', 'split')), may hold values from 0.1 to 1
- solution: float32 [65536, 64], P(('blk', 'split')), may hold values from -6 to 6
- residual: float32 [65536, 64], P(('blk', 'split')), may hold values from -6 to 6
- direction: float32 [65536, 64], P(('blk', 'split')), may hold values from -6 to 6
Outputs:
- solution_out: float32 [65536, 64], P(('blk', 'split'))
- residual_out: float32 [65536, 64], P(('blk', 'split'))
- direction_out: float32 [65536, 64], P(('blk', 'split'))
The draws below stay inside these ranges and needn't reach their ends.
All inputs are finite; a program needn't handle non-finite values.
Results may differ from the reference program's by a relative error of at most 0.0045.
Values may be sent and summed in bfloat16 or wider, within the bound.
A program may use at most 64 MiB of HBM per device.

```python
import math
import jax
import jax.numpy as jnp
from jax import lax

F = 128
COLS = 64
POINTS = 65536


def field_draw(key):
    rising = 0.5 + jnp.arange(POINTS, dtype=jnp.float32) / POINTS
    base = jnp.clip(jax.random.normal(key, (POINTS, COLS), jnp.float32), -4.0, 4.0)
    return base * rising[:, None]


def draw_points(key, part):
    key = jax.random.fold_in(key, 11)
    subkeys = jax.random.split(key, 6)
    per_latent = F // 8
    lat_scale = 3.73 / math.sqrt(F)
    latent = jnp.clip(jax.random.normal(subkeys[0], (POINTS, 8), jnp.float32), -3.0, 3.0)
    jitter = jnp.clip(jax.random.normal(subkeys[1], (POINTS, F), jnp.float32), -4.0, 4.0)
    magnitude = jax.random.uniform(subkeys[2], (F,), jnp.float32, 0.6, 1.4)
    sign_flip = (2 * jax.random.randint(subkeys[3], (F,), 0, 2) - 1).astype(jnp.float32)
    frequency = jax.random.uniform(subkeys[4], (F,), jnp.float32, 1.0, 2.0)
    phases = jax.random.uniform(subkeys[5], (F,), jnp.float32, -3.14159, 3.14159)
    spread = jnp.tile(latent, (1, per_latent))
    values = sign_flip * magnitude * spread + 0.5 * jnp.sin(frequency * spread + phases) + 0.3 * jitter
    return (lat_scale * values).astype(jnp.bfloat16)


def draw_residual(key, part):
    key = jax.random.fold_in(key, 23)
    return field_draw(key)


def draw_direction(key, part):
    key = jax.random.fold_in(key, 37)
    return field_draw(key)


def block_scale(own_key, extent, cuts, smallest, high):
    gain = 1.0
    for position, parts in cuts:
        draws = jax.random.uniform(jax.random.fold_in(jax.random.fold_in(own_key, 6), position), (parts,), jnp.float32, smallest / len(cuts), high / len(cuts))
        gain = gain * jnp.repeat(jnp.exp(draws), extent[position] // parts).reshape((-1,) + (1,) * (len(extent) - 1 - position))
    return gain


def centred(own_key, dims, deviation, limit, cuts=(), kind=jnp.bfloat16):
    entries = jax.random.normal(own_key, dims, jnp.float32) * deviation
    if len(cuts) > 0:
        entries = block_scale(own_key, dims, cuts, -0.22, 0.18) * entries
    return jnp.clip(entries, min=-limit, max=limit).astype(kind)


def setup_inputs(seed: int = 0) -> dict:
    key_list = jax.random.split(jax.random.key(seed), 8)
    points = draw_points(jax.random.fold_in(key_list[7], 71), 0)
    inv_length = jnp.clip(jnp.exp(jax.random.uniform(key_list[1], (F,), jnp.float32, math.log(0.2), math.log(1.0))), 0.2, 1.0)
    amplitude = jnp.clip(jnp.exp(jax.random.uniform(key_list[2], (), jnp.float32, math.log(0.1), math.log(0.4))), 0.1, 0.4)
    noise = jnp.clip(jnp.exp(math.log(1.0) - 2.3025851 * jax.random.uniform(key_list[3], (POINTS,), jnp.float32) ** block_scale(key_list[3], (POINTS,), ((0, 128),), -0.2, 0.2)), 0.1, 1.0)
    solution = centred(key_list[4], (POINTS, COLS), 1.0, 6.0, ((0, 128),), jnp.float32)
    residual = draw_residual(jax.random.fold_in(key_list[7], 71), 0)
    direction = draw_direction(jax.random.fold_in(key_list[7], 71), 0)
    return dict(points=points, inv_length=inv_length, amplitude=amplitude, noise=noise, solution=solution, residual=residual, direction=direction)


def reference(points, inv_length, amplitude, noise, solution, residual, direction):
    scaled = (points.astype(jnp.float32) * inv_length).astype(jnp.bfloat16)
    squares = jnp.sum(jnp.square(scaled.astype(jnp.float32)), axis=1)
    dir_half = direction.astype(jnp.bfloat16)
    block_size = math.gcd(POINTS, 1024)
    row_blocks = scaled.reshape(POINTS // block_size, block_size, F)
    square_blocks = squares.reshape(POINTS // block_size, block_size)

    def row_block(inputs):
        block_rows, block_squares = inputs
        inner = lax.dot_general(block_rows, scaled, (((1,), (1,)), ((), ())), preferred_element_type=jnp.float32)
        distance = jnp.maximum(block_squares[:, None] + squares[None, :] - 2.0 * inner, 0.0)
        kernel = (amplitude * jnp.exp(-0.5 * distance)).astype(jnp.bfloat16)
        return jnp.dot(kernel, dir_half, preferred_element_type=jnp.float32)

    summed = lax.map(row_block, (row_blocks, square_blocks)).reshape(POINTS, COLS)
    image = summed + noise[:, None] * direction
    old_norm = jnp.sum(residual * residual, axis=0)
    curvature = jnp.sum(direction * image, axis=0)
    step_size = old_norm / curvature
    solution_out = solution + step_size * direction
    residual_out = residual - step_size * image
    new_norm = jnp.sum(residual_out * residual_out, axis=0)
    direction_out = residual_out + (new_norm / old_norm) * direction
    return (solution_out, residual_out, direction_out)
```

```python
import functools

import jax
import jax.numpy as jnp
from jax import lax
from jax.experimental import pallas as pl
from jax.experimental.pallas import tpu as pltpu
from jax.sharding import PartitionSpec as P

F32 = jnp.float32
BF16 = jnp.bfloat16
MESH = pl.DeviceIdType.MESH

I_SLOTS = ((0, 0), (0, 1), (1, 0), (3, 0), (2, 0), (1, 1), (3, 1), (2, 1))
J_SLOTS = (
    (0, 0), (0, 1), (0, 3), (1, 0), (3, 0), (0, 2), (2, 0), (1, 1),
    (1, 3), (3, 1), (3, 3), (1, 2), (3, 2), (2, 1), (2, 3), (2, 2),
)
N_I, N_J = len(I_SLOTS), len(J_SLOTS)
LINE_J = range(1, 7)
NEAR_J = range(1, 5)
LINE_I = range(1, 5)
ROWS = 512
FEAT = 128
COLS = 64
TILE = 256
PACK = 32
HALF = (0, TILE + PACK + 2 * COLS)
DIRS = (TILE + PACK, TILE + PACK + 2 * COLS + TILE)
SHIP = 2 * (TILE + 2 * COLS) + PACK
PIECE = ((0, HALF[1]), (HALF[1], SHIP - HALF[1]))
I_SHIP = FEAT + 16

RECTS = (
    (0, 1, 2, 0, 2, "i"),
    (2, 1, 2, 0, 2, "i"),
    (5, 1, 2, 0, 2, "i"),
    (4, 3, 2, 0, 2, "i"),
    (0, 1, 8, 2, 2, "i"),
    (2, 1, 6, 4, 2, "i"),
    (7, -1, 6, 6, 2, "p"),
    (1, -1, 2, 4, 4, "p"),
)
ORDER = [
    (i0 + s * (n % ni if fast == "i" else n // np_), p0 + (n // ni if fast == "i" else n % np_))
    for i0, s, ni, p0, np_, fast in RECTS
    for n in range(ni * np_)
]
PHASE = sum(r[2] * r[4] for r in RECTS[:-2])
UNITS = len(ORDER)
FIRST_I = [min(u for u in range(UNITS) if ORDER[u][0] == k) for k in range(N_I)]
DONE_I = [max(u for u in range(UNITS) if ORDER[u][0] == k) for k in range(N_I)]
FIRST_J = [min(u for u in range(UNITS) if ORDER[u][1] == k // 2) for k in range(N_J)]
BODY = 4
FAR = 3


def i_back(k):
    dx, dc = I_SLOTS[k]
    return I_SLOTS.index(((4 - dx) % 4, dc))


def j_back(k):
    dy, dz = J_SLOTS[k]
    return J_SLOTS.index(((4 - dy) % 4, (4 - dz) % 4))


def place():
    b = lax.axis_index("blk")
    s = lax.axis_index("split")
    return (s % 2) * 2 + (b // 2) % 2, b // 4, s // 2, b % 2


def peer(dx, dy, dz, dc):
    x, y, z, c = place()
    x, y, z, c = (x + dx) % 4, (y + dy) % 4, (z + dz) % 4, (c + dc) % 2
    return {"blk": (y * 2 + x % 2) * 2 + c, "split": z * 2 + x // 2}


def i_peer(k):
    dx, dc = I_SLOTS[k]
    return peer(dx, 0, 0, dc)


def j_peer(k):
    dy, dz = J_SLOTS[k]
    return peer(0, dy, dz, 0)


def three(v):
    hi = v.astype(BF16).astype(F32)
    mid = (v - hi).astype(BF16).astype(F32)
    return hi, mid, v - hi - mid


def marked(b, passes):
    return jnp.right_shift(sum(1 << w for w in passes), b) % 2 == 1


def where_is(u):
    ik = jp = jnp.int32(0)
    start = UNITS
    for i0, s, ni, p0, np_, fast in reversed(RECTS):
        end, start = start, start - ni * np_
        v = u - start
        i, p = (v % ni, v // ni) if fast == "i" else (v // np_, v % np_)
        ik = jnp.where(u < end, i0 + s * i, ik)
        jp = jnp.where(u < end, p0 + p, jp)
    return ik, jp


def kernel(
    points_in, inv_length_in, amplitude, noise_in, sol_in, res_in, dir_in,
    sol_out, res_out, dir_out,
    points, inv_length, noise, sol, res, dirn,
    it, jb, jsq, oacc, kbuf, sbuf, mbuf, fbuf, stat,
    in_sem, i_send, i_recv, j_send, j_recv, f_send, m_recv, r_send, r_recv, a_send, a_recv, b_send, b_recv,
):
    fetch = [
        pltpu.make_async_copy(src, dst, in_sem.at[n])
        for n, (src, dst) in enumerate(
            ((points_in, points), (inv_length_in, inv_length), (dir_in, dirn), (noise_in, noise), (res_in, res), (sol_in, sol))
        )
    ]
    for copy in fetch:
        copy.start()
    barrier = pltpu.get_barrier_semaphore()
    for k in LINE_I:
        pl.semaphore_signal(barrier, inc=1, device_id=i_peer(k), device_id_type=MESH)
    for k in LINE_J:
        pl.semaphore_signal(barrier, inc=1, device_id=j_peer(k), device_id_type=MESH)

    for copy in fetch[:3]:
        copy.wait()
    scaled = (points[...].astype(F32) * inv_length[...]).astype(BF16)
    scaled32 = scaled.astype(F32)
    log_amp = jnp.log(jnp.full((1, ROWS), amplitude[0, 0], F32))
    scaled_t = jnp.transpose(scaled32)
    it[0, pl.ds(0, FEAT), :] = scaled_t.astype(BF16)
    high = -0.5 * jnp.sum(scaled_t * scaled_t, axis=0, keepdims=True) + log_amp
    hi, mid, low = three(high)
    sub = lax.broadcasted_iota(jnp.int32, (16, ROWS), 0) % 8
    pattern = jnp.where(sub < 3, 1.0, jnp.where(sub == 3, hi, jnp.where(sub == 4, mid, jnp.where(sub == 5, low, 0.0))))
    it[0, pl.ds(FEAT, 16), :] = pattern.astype(BF16)
    half = -0.5 * jnp.sum(scaled32 * scaled32, axis=1, keepdims=True)
    hi, mid, low = three(half)
    lane = lax.broadcasted_iota(jnp.int32, (PACK, FEAT), 1)
    group, part = lane // 8, lane % 8
    packed = jnp.zeros((PACK, FEAT), F32)
    for b in range(ROWS // PACK):
        rows = slice(b * PACK, (b + 1) * PACK)
        value = jnp.where(part == 0, hi[rows], jnp.where(part == 1, mid[rows], low[rows]))
        value = jnp.where(part < 3, value, jnp.where(part < 6, 1.0, 0.0))
        packed = jnp.where(group == b, value, packed)
    jb[0, pl.ds(TILE, PACK), :] = packed.astype(BF16)
    for side in range(2):
        jb[0, pl.ds(HALF[side], TILE), :] = scaled[side * TILE : (side + 1) * TILE]
        for b in range(2):
            start = side * TILE + b * FEAT
            jb[0, pl.ds(DIRS[side] + b * COLS, COLS), :] = dirn[:, pl.ds(start, FEAT)].astype(BF16)

    def remote(src, dst, send, recv, to):
        return pltpu.make_async_remote_copy(
            src_ref=src, dst_ref=dst, send_sem=send, recv_sem=recv, device_id=to, device_id_type=MESH
        )

    def i_copy(k):
        back = i_back(k)
        return remote(it.at[0, pl.ds(0, I_SHIP)], it.at[back, pl.ds(0, I_SHIP)], i_send.at[k], i_recv.at[back], i_peer(k))

    def i_pass(k):
        return remote(
            it.at[k, pl.ds(0, I_SHIP)], it.at[k + 3, pl.ds(0, I_SHIP)], i_send.at[k + 3], i_recv.at[k + 3], i_peer(1)
        )

    def j_copy(k, piece):
        back = j_back(k)
        rows = pl.ds(*PIECE[piece])
        return remote(
            jb.at[0, rows], jb.at[back, rows], j_send.at[k, piece], j_recv.at[back, piece], j_peer(k)
        )

    def j_pass(k, n):
        dy, dz = J_SLOTS[k]
        piece = 0 if dz else 1
        to = J_SLOTS.index((n, 0) if dz else (0, n))
        lands = J_SLOTS.index((4 - n, dz) if dz else (dy, 4 - n))
        rows = pl.ds(*PIECE[piece])
        return remote(
            jb.at[k, rows], jb.at[lands, rows], f_send.at[k, n], j_recv.at[lands, piece], j_peer(to)
        )

    def j_line(k):
        dz = J_SLOTS[k][1]
        piece, lands, to = (0 if k in (1, 3) else 1), (5 if dz else 6), j_back(k)
        rows = pl.ds(*PIECE[piece])
        return remote(
            jb.at[k, rows], jb.at[lands, rows], f_send.at[k, 0], j_recv.at[lands, piece], j_peer(to)
        )

    def mix_copy(k):
        return remote(sbuf.at[k], mbuf.at[k - 3], r_send.at[k], m_recv.at[k - 3], i_peer(1))

    def r_copy(k):
        back = i_back(k)
        return remote(sbuf.at[k], fbuf.at[back], r_send.at[k], r_recv.at[back], i_peer(k))

    pl.semaphore_wait(barrier, len(LINE_I) + len(LINE_J))
    for k in LINE_I:
        i_copy(k).start()
    for piece in range(2):
        for k in NEAR_J:
            j_copy(k, piece).start()
    oacc[...] = jnp.zeros_like(oacc)

    def spread(k):
        packed = jb[k, pl.ds(TILE, PACK), :].astype(F32)
        for b in range(ROWS // PACK):
            jsq[k, pl.ds(b * PACK, PACK), :] = jnp.where(group == b, packed, 0.0).astype(BF16)

    spread(0)

    def fill(k):
        two = it[k, pl.ds(FEAT, 16), :]
        for r in range(FEAT + 16, TILE, 16):
            it[k, pl.ds(r, 16), :] = two

    fill(0)

    def want_i(k):
        if k in LINE_I:
            i_copy(i_back(k)).wait_recv()
            if k != 1:
                i_pass(k).start()
        else:
            i_pass(k - 3).wait_recv()
        fill(k)

    def want_j(k, piece):
        j_copy(j_back(k), piece).wait_recv()
        if piece == 0:
            spread(k)
        dy, dz = J_SLOTS[k]
        if k in NEAR_J and piece == (0 if k in (1, 3) else 1):
            j_line(k).start()
        if k in LINE_J and piece == (0 if dz else 1):
            for n in (1, 3):
                j_pass(k, n).start()

    def pass_far(k):
        j_pass(k, 2).start()

    events = {}

    def at(u, *what):
        events.setdefault(u, []).append(what)

    for k in range(1, N_I):
        at((FIRST_I[k] - 1) // BODY, want_i, k)
    for k in range(1, N_J):
        passed = 0 if J_SLOTS[k][1] else 1
        use = (FIRST_J[k] - 1) // BODY
        if k in LINE_J:
            at(min(use, 0 if k < 5 else FAR), want_j, k, passed)
            at(use, want_j, k, 1 - passed)
            at(1 if k in NEAR_J else FAR, pass_far, k)
        else:
            at(use, want_j, k, 0)
            at(use, want_j, k, 1)

    def give(k):
        if k > 4:
            sbuf[k] = oacc[k].astype(BF16)
            mix_copy(k).start()
            return
        if k > 1:
            mix_copy(k + 3).wait_recv()
            sbuf[k] = (oacc[k] + mbuf[k].astype(F32)).astype(BF16)
        else:
            sbuf[k] = oacc[k].astype(BF16)
        r_copy(k).start()

    def work(e00, e01, e10, e11, o00, o01, o10, o11):
        e_acc = ((e00, e01), (e10, e11))
        o_acc = ((o00, o01), (o10, o11))
        ceiling = jnp.log(jnp.full((8, TILE), amplitude[0, 0], F32))[0:1]

        def inner(ik, jp, t):
            for q in range(2):
                pltpu.matmul_push_rhs(it[ik, :, pl.ds(q * TILE, TILE)], 0, q)
            slot, side = 2 * jp + t // 2, t % 2
            rows = jb[slot, pl.ds(HALF[side], TILE), :]
            lhs = jnp.concatenate([rows, jsq[slot, pl.ds(side * TILE, TILE), :]], axis=1)
            for q in range(2):
                pltpu.matmul_acc_lhs(e_acc[q][t % 2], lhs, load_staged_rhs=0)

        def expo(t):
            for q in range(2):
                e = pltpu.matmul_pop(e_acc[q][t % 2])
                kbuf[t % 2, q] = jnp.exp(jnp.minimum(e, ceiling)).astype(BF16)

        def product(jp, t, turn):
            slot, base = 2 * jp + t // 2, DIRS[t % 2]
            lhs = jnp.concatenate([jb[slot, pl.ds(base, COLS), :], jb[slot, pl.ds(base + COLS, COLS), :]], axis=1)
            for q in range(2):
                pltpu.matmul_push_rhs(kbuf[t % 2, q], 1, q)
            for q in range(2):
                pltpu.matmul_acc_lhs(o_acc[q][turn], lhs, load_staged_rhs=1)

        def collect(ik, turn):
            for q in range(2):
                oacc[ik, :, pl.ds(q * TILE, TILE)] += pltpu.matmul_pop(o_acc[q][turn])

        for what in events.pop(-1, []):
            what[0](*what[1:])
        inner(0, 0, 0)
        inner(0, 0, 1)
        expo(0)

        @pl.loop(0, UNITS // BODY)
        def _(b):
            @pl.when(marked(b, events))
            def _():
                for when, actions in sorted(events.items()):

                    @pl.when(b == when)
                    def _(actions=actions):
                        for what in actions:
                            what[0](*what[1:])

            for n in range(BODY):
                u = b * BODY + n
                ik, jp = where_is(u)
                ik_next, jp_next = where_is(jnp.minimum(u + 1, UNITS - 1))
                inner(ik, jp, 2)
                expo(1)
                product(jp, 0, n % 2)
                inner(ik, jp, 3)
                expo(2)
                collect(where_is(jnp.maximum(u - 1, 0))[0], 1 - n % 2)
                product(jp, 1, n % 2)
                inner(ik_next, jp_next, 0)
                expo(3)
                product(jp, 2, n % 2)
                inner(ik_next, jp_next, 1)
                expo(0)
                product(jp, 3, n % 2)

            @pl.when(b >= PHASE // BODY)
            def _():
                collect(where_is(b * BODY + BODY - 1)[0], (BODY - 1) % 2)
                for k in range(N_I - 1, 0, -1):
                    pl.when(b == DONE_I[k] // BODY)(functools.partial(give, k))

        for q in range(2):
            spare = pltpu.matmul_pop(e_acc[q][1])
            stat[1, 0] = spare[0:8, 0:FEAT]

    pl.run_scoped(
        work,
        *[pltpu.ACC(q)((TILE, TILE), F32) for q in (0, 0, 1, 1)],
        *[pltpu.ACC(q)((COLS, TILE), F32) for q in (0, 0, 1, 1)],
    )

    for copy in fetch[3:]:
        copy.wait()
    d = dirn[...]
    r = res[...]
    image = noise[...] * d + oacc[0]
    for k in LINE_I:
        r_copy(i_back(k)).wait_recv()
        image = image + fbuf[k].astype(F32)
    lane = lax.broadcasted_iota(jnp.int32, (COLS, FEAT), 1)
    sums = jnp.zeros((COLS, FEAT), F32)
    for n, v in enumerate((r * r, d * image, r * image, image * image)):
        sums = jnp.where(lane == n, jnp.sum(v, axis=1, keepdims=True), sums)
    sums = jnp.transpose(jnp.concatenate([sums, jnp.zeros((FEAT - COLS, FEAT), F32)], axis=0))
    stat[0, 0] = sums[0:8]

    def a_copy(k):
        back = j_back(k)
        return remote(stat.at[0, 0], stat.at[0, back], a_send.at[k], a_recv.at[back], j_peer(k))

    def b_copy(k):
        back = i_back(k)
        return remote(stat.at[1, 0], stat.at[1, back], b_send.at[k], b_recv.at[back], i_peer(k))

    for k in range(1, N_J):
        a_copy(k).start()
    for k in range(1, N_J):
        a_copy(j_back(k)).wait_recv()
    stat[1, 0] = jnp.sum(stat[0], axis=0)
    for k in range(1, N_I):
        b_copy(k).start()
    for k in range(1, N_I):
        b_copy(i_back(k)).wait_recv()
    total = jnp.sum(stat[1, pl.ds(0, N_I)], axis=0)
    total = jnp.transpose(jnp.concatenate([total, jnp.zeros((FEAT - 8, FEAT), F32)], axis=0))
    old_norm, curvature, cross, square = [total[:COLS, n : n + 1] for n in range(4)]
    step = old_norm / curvature
    new_norm = jnp.maximum(old_norm - 2.0 * step * cross + step * step * square, 0.0)
    r_new = r - step * image
    sol_out[...] = sol[...] + step * d
    res_out[...] = r_new
    dir_out[...] = r_new + (new_norm / old_norm) * d

    for k in LINE_I:
        i_copy(k).wait_send()
    for k in (2, 3, 4):
        i_pass(k).wait_send()
    for k in LINE_J:
        if k in NEAR_J:
            for piece in range(2):
                j_copy(k, piece).wait_send()
            j_line(k).wait_send()
        for n in (1, 3, 2):
            j_pass(k, n).wait_send()
    for k in range(1, N_I):
        (mix_copy if k > 4 else r_copy)(k).wait_send()
        b_copy(k).wait_send()
    for k in range(1, N_J):
        a_copy(k).wait_send()


def per_device(points, inv_length, amplitude, noise, sol, res, dirn):
    vmem = pl.BlockSpec(memory_space=pltpu.VMEM)
    hbm = pl.BlockSpec(memory_space=pltpu.HBM)
    out = jax.ShapeDtypeStruct((COLS, ROWS), F32)
    dma = pltpu.SemaphoreType.DMA
    outs = pl.pallas_call(
        kernel,
        out_shape=(out, out, out),
        in_specs=[hbm, hbm, pl.BlockSpec(memory_space=pltpu.SMEM), hbm, hbm, hbm, hbm],
        out_specs=(vmem, vmem, vmem),
        scratch_shapes=[
            pltpu.VMEM((ROWS, FEAT), BF16),
            pltpu.VMEM((1, FEAT), F32),
            pltpu.VMEM((1, ROWS), F32),
            pltpu.VMEM((COLS, ROWS), F32),
            pltpu.VMEM((COLS, ROWS), F32),
            pltpu.VMEM((COLS, ROWS), F32),
            pltpu.VMEM((N_I, TILE, ROWS), BF16),
            pltpu.VMEM((N_J, SHIP, FEAT), BF16),
            pltpu.VMEM((N_J, ROWS, FEAT), BF16),
            pltpu.VMEM((N_I, COLS, ROWS), F32),
            pltpu.VMEM((2, 2, TILE, TILE), BF16),
            pltpu.VMEM((N_I, COLS, ROWS), BF16),
            pltpu.VMEM((5, COLS, ROWS), BF16),
            pltpu.VMEM((5, COLS, ROWS), BF16),
            pltpu.VMEM((2, N_J, 8, FEAT), F32),
            dma((6,)),
            dma((N_I,)),
            dma((N_I,)),
            dma((N_J, 2)),
            dma((N_J, 2)),
            dma((7, 4)),
            dma((5,)),
            dma((N_I,)),
            dma((5,)),
            dma((N_J,)),
            dma((N_J,)),
            dma((N_I,)),
            dma((N_I,)),
        ],
        compiler_params=pltpu.CompilerParams(
            collective_id=0, has_side_effects=True, vmem_limit_bytes=64 * 1024 * 1024
        ),
        name="cg_step",
    )(points, inv_length.reshape(1, -1), amplitude.reshape(1, 1), noise.reshape(1, -1), sol.T, res.T, dirn.T)
    return tuple(v.T for v in outs)


def solution(mesh):
    placed = (
        P(("blk", "split"), None),
        P(),
        P(),
        P(("blk", "split")),
        P(("blk", "split"), None),
        P(("blk", "split"), None),
        P(("blk", "split"), None),
    )

    def whole(*args):
        with jax.sharding.use_abstract_mesh(mesh.abstract_mesh):
            return jax.shard_map(
                per_device,
                mesh=mesh,
                in_specs=placed,
                out_specs=(P(("blk", "split"), None),) * 3,
                check_vma=False,
            )(*args)

    return whole
```

```python
import functools

import jax
import jax.numpy as jnp
from jax import lax
from jax.experimental import pallas as pl
from jax.experimental.pallas import tpu as pltpu
from jax.sharding import PartitionSpec as P

F32 = jnp.float32
BF16 = jnp.bfloat16
MESH = pl.DeviceIdType.MESH

I_SLOTS = ((0, 0), (0, 1), (1, 0), (3, 0), (2, 0), (1, 1), (3, 1), (2, 1))
J_SLOTS = (
    (0, 0), (0, 1), (0, 3), (1, 0), (3, 0), (0, 2), (2, 0), (1, 1),
    (1, 3), (3, 1), (3, 3), (1, 2), (3, 2), (2, 1), (2, 3), (2, 2),
)
N_I, N_J = len(I_SLOTS), len(J_SLOTS)
LINE_J = range(1, 7)
NEAR_J = range(1, 5)
LINE_I = range(1, 5)
ROWS = 512
FEAT = 128
COLS = 64
TILE = 256
PACK = 32
HALF = (0, TILE + PACK + 2 * COLS)
DIRS = (TILE + PACK, TILE + PACK + 2 * COLS + TILE)
SHIP = 2 * (TILE + 2 * COLS) + PACK
PIECE = ((0, HALF[1]), (HALF[1], SHIP - HALF[1]))
I_SHIP = FEAT + 16

RECTS = (
    (0, 1, 2, 0, 2, "i"),
    (2, 1, 2, 0, 2, "i"),
    (5, 1, 2, 0, 2, "i"),
    (4, 3, 2, 0, 2, "i"),
    (0, 1, 8, 2, 2, "i"),
    (2, 1, 6, 4, 2, "i"),
    (7, -1, 6, 6, 2, "p"),
    (1, -1, 2, 4, 4, "p"),
)
ORDER = [
    (i0 + s * (n % ni if fast == "i" else n // np_), p0 + (n // ni if fast == "i" else n % np_))
    for i0, s, ni, p0, np_, fast in RECTS
    for n in range(ni * np_)
]
PHASE = sum(r[2] * r[4] for r in RECTS[:-2])
UNITS = len(ORDER)
FIRST_I = [min(u for u in range(UNITS) if ORDER[u][0] == k) for k in range(N_I)]
DONE_I = [max(u for u in range(UNITS) if ORDER[u][0] == k) for k in range(N_I)]
FIRST_J = [min(u for u in range(UNITS) if ORDER[u][1] == k // 2) for k in range(N_J)]
BODY = 4
FAR = 3


def i_back(k):
    dx, dc = I_SLOTS[k]
    return I_SLOTS.index(((4 - dx) % 4, dc))


def j_back(k):
    dy, dz = J_SLOTS[k]
    return J_SLOTS.index(((4 - dy) % 4, (4 - dz) % 4))


def place():
    b = lax.axis_index("blk")
    s = lax.axis_index("split")
    return (s % 2) * 2 + (b // 2) % 2, b // 4, s // 2, b % 2


def peer(dx, dy, dz, dc):
    x, y, z, c = place()
    x, y, z, c = (x + dx) % 4, (y + dy) % 4, (z + dz) % 4, (c + dc) % 2
    return {"blk": (y * 2 + x % 2) * 2 + c, "split": z * 2 + x // 2}


def i_peer(k):
    dx, dc = I_SLOTS[k]
    return peer(dx, 0, 0, dc)


def j_peer(k):
    dy, dz = J_SLOTS[k]
    return peer(0, dy, dz, 0)


def three(v):
    hi = v.astype(BF16).astype(F32)
    mid = (v - hi).astype(BF16).astype(F32)
    return hi, mid, v - hi - mid


def marked(b, passes):
    return jnp.right_shift(sum(1 << w for w in passes), b) % 2 == 1


def where_is(u):
    ik = jp = jnp.int32(0)
    start = UNITS
    for i0, s, ni, p0, np_, fast in reversed(RECTS):
        end, start = start, start - ni * np_
        v = u - start
        i, p = (v % ni, v // ni) if fast == "i" else (v // np_, v % np_)
        ik = jnp.where(u < end, i0 + s * i, ik)
        jp = jnp.where(u < end, p0 + p, jp)
    return ik, jp


def kernel(
    points_in, inv_length_in, amplitude, noise_in, sol_in, res_in, dir_in,
    out,
    points, inv_length, noise, sol, res, dirn,
    it, jb, jsq, oacc, kbuf, sbuf, mbuf, fbuf, stat,
    in_sem, i_send, i_recv, j_send, j_recv, f_send, m_recv, r_send, r_recv, a_send, a_recv, b_send, b_recv,
):
    fetch = [
        pltpu.make_async_copy(src, dst, in_sem.at[n])
        for n, (src, dst) in enumerate(
            ((points_in, points), (inv_length_in, inv_length), (dir_in, dirn), (noise_in, noise), (res_in, res), (sol_in, sol))
        )
    ]
    for copy in fetch:
        copy.start()
    barrier = pltpu.get_barrier_semaphore()
    for k in LINE_I:
        pl.semaphore_signal(barrier, inc=1, device_id=i_peer(k), device_id_type=MESH)
    for k in LINE_J:
        pl.semaphore_signal(barrier, inc=1, device_id=j_peer(k), device_id_type=MESH)

    for copy in fetch[:3]:
        copy.wait()
    scaled = (points[...].astype(F32) * inv_length[...]).astype(BF16)
    scaled32 = scaled.astype(F32)
    log_amp = jnp.log(jnp.full((1, ROWS), amplitude[0, 0], F32))
    scaled_t = jnp.transpose(scaled32)
    it[0, pl.ds(0, FEAT), :] = scaled_t.astype(BF16)
    high = -0.5 * jnp.sum(scaled_t * scaled_t, axis=0, keepdims=True) + log_amp
    hi, mid, low = three(high)
    sub = lax.broadcasted_iota(jnp.int32, (16, ROWS), 0) % 8
    pattern = jnp.where(sub < 3, 1.0, jnp.where(sub == 3, hi, jnp.where(sub == 4, mid, jnp.where(sub == 5, low, 0.0))))
    it[0, pl.ds(FEAT, 16), :] = pattern.astype(BF16)
    half = -0.5 * jnp.sum(scaled32 * scaled32, axis=1, keepdims=True)
    hi, mid, low = three(half)
    lane = lax.broadcasted_iota(jnp.int32, (PACK, FEAT), 1)
    group, part = lane // 8, lane % 8
    packed = jnp.zeros((PACK, FEAT), F32)
    for b in range(ROWS // PACK):
        rows = slice(b * PACK, (b + 1) * PACK)
        value = jnp.where(part == 0, hi[rows], jnp.where(part == 1, mid[rows], low[rows]))
        value = jnp.where(part < 3, value, jnp.where(part < 6, 1.0, 0.0))
        packed = jnp.where(group == b, value, packed)
    jb[0, pl.ds(TILE, PACK), :] = packed.astype(BF16)
    for side in range(2):
        jb[0, pl.ds(HALF[side], TILE), :] = scaled[side * TILE : (side + 1) * TILE]
        for b in range(2):
            start = side * TILE + b * FEAT
            jb[0, pl.ds(DIRS[side] + b * COLS, COLS), :] = dirn[:, pl.ds(start, FEAT)].astype(BF16)

    def remote(src, dst, send, recv, to):
        return pltpu.make_async_remote_copy(
            src_ref=src, dst_ref=dst, send_sem=send, recv_sem=recv, device_id=to, device_id_type=MESH
        )

    def i_copy(k):
        back = i_back(k)
        return remote(it.at[0, pl.ds(0, I_SHIP)], it.at[back, pl.ds(0, I_SHIP)], i_send.at[k], i_recv.at[back], i_peer(k))

    def i_pass(k):
        return remote(
            it.at[k, pl.ds(0, I_SHIP)], it.at[k + 3, pl.ds(0, I_SHIP)], i_send.at[k + 3], i_recv.at[k + 3], i_peer(1)
        )

    def j_copy(k, piece):
        back = j_back(k)
        rows = pl.ds(*PIECE[piece])
        return remote(
            jb.at[0, rows], jb.at[back, rows], j_send.at[k, piece], j_recv.at[back, piece], j_peer(k)
        )

    def j_pass(k, n):
        dy, dz = J_SLOTS[k]
        piece = 0 if dz else 1
        to = J_SLOTS.index((n, 0) if dz else (0, n))
        lands = J_SLOTS.index((4 - n, dz) if dz else (dy, 4 - n))
        rows = pl.ds(*PIECE[piece])
        return remote(
            jb.at[k, rows], jb.at[lands, rows], f_send.at[k, n], j_recv.at[lands, piece], j_peer(to)
        )

    def j_line(k):
        dz = J_SLOTS[k][1]
        piece, lands, to = (0 if k in (1, 3) else 1), (5 if dz else 6), j_back(k)
        rows = pl.ds(*PIECE[piece])
        return remote(
            jb.at[k, rows], jb.at[lands, rows], f_send.at[k, 0], j_recv.at[lands, piece], j_peer(to)
        )

    def mix_copy(k):
        return remote(sbuf.at[k], mbuf.at[k - 3], r_send.at[k], m_recv.at[k - 3], i_peer(1))

    def r_copy(k):
        back = i_back(k)
        return remote(sbuf.at[k], fbuf.at[back], r_send.at[k], r_recv.at[back], i_peer(k))

    pl.semaphore_wait(barrier, len(LINE_I) + len(LINE_J))
    for k in NEAR_J:
        j_copy(k, 0).start()
    for k in LINE_I[:3]:
        i_copy(k).start()
    for k in NEAR_J:
        j_copy(k, 1).start()
    for k in LINE_I[3:]:
        i_copy(k).start()
    oacc[...] = jnp.zeros_like(oacc)

    def spread(k):
        packed = jb[k, pl.ds(TILE, PACK), :].astype(F32)
        for b in range(ROWS // PACK):
            jsq[k, pl.ds(b * PACK, PACK), :] = jnp.where(group == b, packed, 0.0).astype(BF16)

    spread(0)

    def fill(k):
        two = it[k, pl.ds(FEAT, 16), :]
        for r in range(FEAT + 16, TILE, 16):
            it[k, pl.ds(r, 16), :] = two

    fill(0)

    def want_i(k):
        if k in LINE_I:
            i_copy(i_back(k)).wait_recv()
            if k != 1:
                i_pass(k).start()
        else:
            i_pass(k - 3).wait_recv()
        fill(k)

    def want_j(k, piece):
        j_copy(j_back(k), piece).wait_recv()
        if piece == 0:
            spread(k)
        dy, dz = J_SLOTS[k]
        if k in NEAR_J and piece == (0 if k in (1, 3) else 1):
            j_line(k).start()
        if k in LINE_J and piece == (0 if dz else 1):
            for n in (1, 3):
                j_pass(k, n).start()

    def pass_far(k):
        j_pass(k, 2).start()

    events = {}

    def at(u, *what):
        events.setdefault(u, []).append(what)

    for k in range(1, N_I):
        at((FIRST_I[k] - 1) // BODY, want_i, k)
    for k in range(1, N_J):
        passed = 0 if J_SLOTS[k][1] else 1
        use = (FIRST_J[k] - 1) // BODY
        if k in LINE_J:
            at(min(use, 0 if k < 5 else FAR), want_j, k, passed)
            at(use, want_j, k, 1 - passed)
            at(3 if k in NEAR_J else FAR + 2, pass_far, k)
        else:
            at(use, want_j, k, 0)
            at(use, want_j, k, 1)

    def give(k):
        if k > 4:
            sbuf[k] = oacc[k].astype(BF16)
            mix_copy(k).start()
            return
        if k > 1:
            mix_copy(k + 3).wait_recv()
            sbuf[k] = (oacc[k] + mbuf[k].astype(F32)).astype(BF16)
        else:
            sbuf[k] = oacc[k].astype(BF16)
        r_copy(k).start()

    def work(e00, e01, e10, e11, o00, o01, o10, o11):
        e_acc = ((e00, e01), (e10, e11))
        o_acc = ((o00, o01), (o10, o11))
        ceiling = jnp.log(jnp.full((8, TILE), amplitude[0, 0], F32))[0:1]

        def inner(ik, jp, t):
            for q in range(2):
                pltpu.matmul_push_rhs(it[ik, :, pl.ds(q * TILE, TILE)], 0, q)
            slot, side = 2 * jp + t // 2, t % 2
            rows = jb[slot, pl.ds(HALF[side], TILE), :]
            lhs = jnp.concatenate([rows, jsq[slot, pl.ds(side * TILE, TILE), :]], axis=1)
            for q in range(2):
                pltpu.matmul_acc_lhs(e_acc[q][t % 2], lhs, load_staged_rhs=0)

        def expo(t):
            for q in range(2):
                e = pltpu.matmul_pop(e_acc[q][t % 2])
                kbuf[t % 2, q] = jnp.exp(jnp.minimum(e, ceiling)).astype(BF16)

        def product(jp, t, turn):
            slot, base = 2 * jp + t // 2, DIRS[t % 2]
            lhs = jnp.concatenate([jb[slot, pl.ds(base, COLS), :], jb[slot, pl.ds(base + COLS, COLS), :]], axis=1)
            for q in range(2):
                pltpu.matmul_push_rhs(kbuf[t % 2, q], 1, q)
            for q in range(2):
                pltpu.matmul_acc_lhs(o_acc[q][turn], lhs, load_staged_rhs=1)

        def collect(ik, turn):
            for q in range(2):
                oacc[ik, :, pl.ds(q * TILE, TILE)] += pltpu.matmul_pop(o_acc[q][turn])

        for what in events.pop(-1, []):
            what[0](*what[1:])
        inner(0, 0, 0)
        inner(0, 0, 1)
        expo(0)

        @pl.loop(0, UNITS // BODY)
        def _(b):
            @pl.when(marked(b, events))
            def _():
                for when, actions in sorted(events.items()):

                    @pl.when(b == when)
                    def _(actions=actions):
                        for what in actions:
                            what[0](*what[1:])

            for n in range(BODY):
                u = b * BODY + n
                ik, jp = where_is(u)
                ik_next, jp_next = where_is(jnp.minimum(u + 1, UNITS - 1))
                inner(ik, jp, 2)
                expo(1)
                product(jp, 0, n % 2)
                inner(ik, jp, 3)
                expo(2)
                collect(where_is(jnp.maximum(u - 1, 0))[0], 1 - n % 2)
                product(jp, 1, n % 2)
                inner(ik_next, jp_next, 0)
                expo(3)
                product(jp, 2, n % 2)
                inner(ik_next, jp_next, 1)
                expo(0)
                product(jp, 3, n % 2)

            @pl.when(b >= PHASE // BODY)
            def _():
                collect(where_is(b * BODY + BODY - 1)[0], (BODY - 1) % 2)
                for k in range(N_I - 1, 0, -1):
                    pl.when(b == DONE_I[k] // BODY)(functools.partial(give, k))

        for q in range(2):
            spare = pltpu.matmul_pop(e_acc[q][1])
            stat[1, 0] = spare[0:8, 0:FEAT]

    pl.run_scoped(
        work,
        *[pltpu.ACC(q)((TILE, TILE), F32) for q in (0, 0, 1, 1)],
        *[pltpu.ACC(q)((COLS, TILE), F32) for q in (0, 0, 1, 1)],
    )

    for copy in fetch[3:]:
        copy.wait()
    d = dirn[...]
    r = res[...]
    image = noise[...] * d + oacc[0]
    for k in LINE_I:
        r_copy(i_back(k)).wait_recv()
        image = image + fbuf[k].astype(F32)
    lane = lax.broadcasted_iota(jnp.int32, (COLS, FEAT), 1)
    sums = jnp.zeros((COLS, FEAT), F32)
    for n, v in enumerate((r * r, d * image, r * image, image * image)):
        sums = jnp.where(lane == n, jnp.sum(v, axis=1, keepdims=True), sums)
    sums = jnp.transpose(jnp.concatenate([sums, jnp.zeros((FEAT - COLS, FEAT), F32)], axis=0))
    stat[0, 0] = sums[0:8]

    def a_copy(k):
        back = j_back(k)
        return remote(stat.at[0, 0], stat.at[0, back], a_send.at[k], a_recv.at[back], j_peer(k))

    def b_copy(k):
        back = i_back(k)
        return remote(stat.at[1, 0], stat.at[1, back], b_send.at[k], b_recv.at[back], i_peer(k))

    for k in range(1, N_J):
        a_copy(k).start()
    for k in LINE_I:
        i_copy(k).wait_send()
    for k in (2, 3, 4):
        i_pass(k).wait_send()
    for k in LINE_J:
        if k in NEAR_J:
            for piece in range(2):
                j_copy(k, piece).wait_send()
            j_line(k).wait_send()
        for n in (1, 3, 2):
            j_pass(k, n).wait_send()
    for k in range(1, N_I):
        (mix_copy if k > 4 else r_copy)(k).wait_send()
    for k in range(1, N_J):
        a_copy(j_back(k)).wait_recv()
    stat[1, 0] = jnp.sum(stat[0], axis=0)
    for k in range(1, N_I):
        b_copy(k).start()
    for k in range(1, N_J):
        a_copy(k).wait_send()
    for k in range(1, N_I):
        b_copy(i_back(k)).wait_recv()
    total = jnp.sum(stat[1, pl.ds(0, N_I)], axis=0)
    total = jnp.transpose(jnp.concatenate([total, jnp.zeros((FEAT - 8, FEAT), F32)], axis=0))
    old_norm, curvature, cross, square = [total[:COLS, n : n + 1] for n in range(4)]
    step = old_norm / curvature
    new_norm = jnp.maximum(old_norm - 2.0 * step * cross + step * step * square, 0.0)
    r_new = r - step * image
    out[0] = sol[...] + step * d
    out[1] = r_new
    out[2] = r_new + (new_norm / old_norm) * d

    for k in range(1, N_I):
        b_copy(k).wait_send()


def per_device(points, inv_length, amplitude, noise, sol, res, dirn):
    vmem = pl.BlockSpec(memory_space=pltpu.VMEM)
    hbm = pl.BlockSpec(memory_space=pltpu.HBM)
    out = jax.ShapeDtypeStruct((3, COLS, ROWS), F32)
    dma = pltpu.SemaphoreType.DMA
    outs = pl.pallas_call(
        kernel,
        out_shape=out,
        in_specs=[hbm, hbm, pl.BlockSpec(memory_space=pltpu.SMEM), hbm, hbm, hbm, hbm],
        out_specs=vmem,
        scratch_shapes=[
            pltpu.VMEM((ROWS, FEAT), BF16),
            pltpu.VMEM((1, FEAT), F32),
            pltpu.VMEM((1, ROWS), F32),
            pltpu.VMEM((COLS, ROWS), F32),
            pltpu.VMEM((COLS, ROWS), F32),
            pltpu.VMEM((COLS, ROWS), F32),
            pltpu.VMEM((N_I, TILE, ROWS), BF16),
            pltpu.VMEM((N_J, SHIP, FEAT), BF16),
            pltpu.VMEM((N_J, ROWS, FEAT), BF16),
            pltpu.VMEM((N_I, COLS, ROWS), F32),
            pltpu.VMEM((2, 2, TILE, TILE), BF16),
            pltpu.VMEM((N_I, COLS, ROWS), BF16),
            pltpu.VMEM((5, COLS, ROWS), BF16),
            pltpu.VMEM((5, COLS, ROWS), BF16),
            pltpu.VMEM((2, N_J, 8, FEAT), F32),
            dma((6,)),
            dma((N_I,)),
            dma((N_I,)),
            dma((N_J, 2)),
            dma((N_J, 2)),
            dma((7, 4)),
            dma((5,)),
            dma((N_I,)),
            dma((5,)),
            dma((N_J,)),
            dma((N_J,)),
            dma((N_I,)),
            dma((N_I,)),
        ],
        compiler_params=pltpu.CompilerParams(
            collective_id=0, has_side_effects=True, vmem_limit_bytes=64 * 1024 * 1024
        ),
        name="cg_step",
    )(points, inv_length.reshape(1, -1), amplitude.reshape(1, 1), noise.reshape(1, -1), sol.T, res.T, dirn.T)
    return outs[0].T, outs[1].T, outs[2].T


def solution(mesh):
    placed = (
        P(("blk", "split"), None),
        P(),
        P(),
        P(("blk", "split")),
        P(("blk", "split"), None),
        P(("blk", "split"), None),
        P(("blk", "split"), None),
    )

    def whole(*args):
        with jax.sharding.use_abstract_mesh(mesh.abstract_mesh):
            return jax.shard_map(
                per_device,
                mesh=mesh,
                in_specs=placed,
                out_specs=(P(("blk", "split"), None),) * 3,
                check_vma=False,
            )(*args)

    return whole
```

```python
import functools

import jax
import jax.numpy as jnp
from jax import lax
from jax.experimental import pallas as pl
from jax.experimental.pallas import tpu as pltpu
from jax.sharding import PartitionSpec as P

F32 = jnp.float32
BF16 = jnp.bfloat16
MESH = pl.DeviceIdType.MESH

I_SLOTS = ((0, 0), (0, 1), (1, 0), (3, 0), (2, 0), (1, 1), (3, 1), (2, 1))
J_SLOTS = (
    (0, 0), (0, 1), (0, 3), (1, 0), (3, 0), (0, 2), (2, 0), (1, 1),
    (1, 3), (3, 1), (3, 3), (1, 2), (3, 2), (2, 1), (2, 3), (2, 2),
)
N_I, N_J = len(I_SLOTS), len(J_SLOTS)
LINE_J = range(1, 7)
NEAR_J = range(1, 5)
LINE_I = range(1, 5)
ROWS = 512
FEAT = 128
COLS = 64
TILE = 256
PACK = 32
HALF = (0, TILE + PACK + 2 * COLS)
DIRS = (TILE + PACK, TILE + PACK + 2 * COLS + TILE)
SHIP = 2 * (TILE + 2 * COLS) + PACK
PIECE = ((0, HALF[1]), (HALF[1], SHIP - HALF[1]))
I_SHIP = FEAT + 16

RECTS = (
    (0, 1, 2, 0, 2, "i"),
    (2, 1, 2, 0, 2, "i"),
    (5, 1, 2, 0, 2, "i"),
    (4, 3, 2, 0, 2, "i"),
    (0, 1, 8, 2, 2, "i"),
    (2, 1, 6, 4, 2, "i"),
    (7, -1, 6, 6, 2, "p"),
    (1, -1, 2, 4, 4, "p"),
)
ORDER = [
    (i0 + s * (n % ni if fast == "i" else n // np_), p0 + (n // ni if fast == "i" else n % np_))
    for i0, s, ni, p0, np_, fast in RECTS
    for n in range(ni * np_)
]
PHASE = sum(r[2] * r[4] for r in RECTS[:-2])
UNITS = len(ORDER)
FIRST_I = [min(u for u in range(UNITS) if ORDER[u][0] == k) for k in range(N_I)]
DONE_I = [max(u for u in range(UNITS) if ORDER[u][0] == k) for k in range(N_I)]
FIRST_J = [min(u for u in range(UNITS) if ORDER[u][1] == k // 2) for k in range(N_J)]
BODY = 4
FAR = 3


def i_back(k):
    dx, dc = I_SLOTS[k]
    return I_SLOTS.index(((4 - dx) % 4, dc))


def j_back(k):
    dy, dz = J_SLOTS[k]
    return J_SLOTS.index(((4 - dy) % 4, (4 - dz) % 4))


def place():
    b = lax.axis_index("blk")
    s = lax.axis_index("split")
    return (s % 2) * 2 + (b // 2) % 2, b // 4, s // 2, b % 2


def peer(dx, dy, dz, dc):
    x, y, z, c = place()
    x, y, z, c = (x + dx) % 4, (y + dy) % 4, (z + dz) % 4, (c + dc) % 2
    return {"blk": (y * 2 + x % 2) * 2 + c, "split": z * 2 + x // 2}


def i_peer(k):
    dx, dc = I_SLOTS[k]
    return peer(dx, 0, 0, dc)


def j_peer(k):
    dy, dz = J_SLOTS[k]
    return peer(0, dy, dz, 0)


def three(v):
    hi = v.astype(BF16).astype(F32)
    mid = (v - hi).astype(BF16).astype(F32)
    return hi, mid, v - hi - mid


def marked(b, passes):
    return jnp.right_shift(sum(1 << w for w in passes), b) % 2 == 1


def where_is(u):
    ik = jp = jnp.int32(0)
    start = UNITS
    for i0, s, ni, p0, np_, fast in reversed(RECTS):
        end, start = start, start - ni * np_
        v = u - start
        i, p = (v % ni, v // ni) if fast == "i" else (v // np_, v % np_)
        ik = jnp.where(u < end, i0 + s * i, ik)
        jp = jnp.where(u < end, p0 + p, jp)
    return ik, jp


def kernel(
    points_in, inv_length_in, amplitude, noise_in, sol_in, res_in, dir_in,
    out,
    points, inv_length, noise, sol, res, dirn,
    it, jb, jsq, oacc, kbuf, sbuf, mbuf, fbuf, stat,
    in_sem, i_send, i_recv, j_send, j_recv, f_send, m_recv, r_send, r_recv, a_send, a_recv, b_send, b_recv,
):
    fetch = [
        pltpu.make_async_copy(src, dst, in_sem.at[n])
        for n, (src, dst) in enumerate(
            ((points_in, points), (inv_length_in, inv_length), (dir_in, dirn), (noise_in, noise), (res_in, res), (sol_in, sol))
        )
    ]
    for copy in fetch:
        copy.start()
    barrier = pltpu.get_barrier_semaphore()
    for k in LINE_I:
        pl.semaphore_signal(barrier, inc=1, device_id=i_peer(k), device_id_type=MESH)
    for k in LINE_J:
        pl.semaphore_signal(barrier, inc=1, device_id=j_peer(k), device_id_type=MESH)

    for copy in fetch[:3]:
        copy.wait()
    scaled = (points[...].astype(F32) * inv_length[...]).astype(BF16)
    scaled32 = scaled.astype(F32)
    log_amp = jnp.log(jnp.full((1, ROWS), amplitude[0, 0], F32))
    scaled_t = jnp.transpose(scaled32)
    it[0, pl.ds(0, FEAT), :] = scaled_t.astype(BF16)
    high = -0.5 * jnp.sum(scaled_t * scaled_t, axis=0, keepdims=True) + log_amp
    hi, mid, low = three(high)
    sub = lax.broadcasted_iota(jnp.int32, (16, ROWS), 0) % 8
    pattern = jnp.where(sub < 3, 1.0, jnp.where(sub == 3, hi, jnp.where(sub == 4, mid, jnp.where(sub == 5, low, 0.0))))
    it[0, pl.ds(FEAT, 16), :] = pattern.astype(BF16)
    half = -0.5 * jnp.sum(scaled32 * scaled32, axis=1, keepdims=True)
    hi, mid, low = three(half)
    lane = lax.broadcasted_iota(jnp.int32, (PACK, FEAT), 1)
    group, part = lane // 8, lane % 8
    packed = jnp.zeros((PACK, FEAT), F32)
    for b in range(ROWS // PACK):
        rows = slice(b * PACK, (b + 1) * PACK)
        value = jnp.where(part == 0, hi[rows], jnp.where(part == 1, mid[rows], low[rows]))
        value = jnp.where(part < 3, value, jnp.where(part < 6, 1.0, 0.0))
        packed = jnp.where(group == b, value, packed)
    jb[0, pl.ds(TILE, PACK), :] = packed.astype(BF16)
    for side in range(2):
        jb[0, pl.ds(HALF[side], TILE), :] = scaled[side * TILE : (side + 1) * TILE]
        for b in range(2):
            start = side * TILE + b * FEAT
            jb[0, pl.ds(DIRS[side] + b * COLS, COLS), :] = dirn[:, pl.ds(start, FEAT)].astype(BF16)

    def remote(src, dst, send, recv, to):
        return pltpu.make_async_remote_copy(
            src_ref=src, dst_ref=dst, send_sem=send, recv_sem=recv, device_id=to, device_id_type=MESH
        )

    def i_copy(k):
        back = i_back(k)
        return remote(it.at[0, pl.ds(0, I_SHIP)], it.at[back, pl.ds(0, I_SHIP)], i_send.at[k], i_recv.at[back], i_peer(k))

    def i_pass(k):
        return remote(
            it.at[k, pl.ds(0, I_SHIP)], it.at[k + 3, pl.ds(0, I_SHIP)], i_send.at[k + 3], i_recv.at[k + 3], i_peer(1)
        )

    def j_copy(k, piece):
        back = j_back(k)
        rows = pl.ds(*PIECE[piece])
        return remote(
            jb.at[0, rows], jb.at[back, rows], j_send.at[k, piece], j_recv.at[back, piece], j_peer(k)
        )

    def j_pass(k, n):
        dy, dz = J_SLOTS[k]
        piece = 0 if dz else 1
        to = J_SLOTS.index((n, 0) if dz else (0, n))
        lands = J_SLOTS.index((4 - n, dz) if dz else (dy, 4 - n))
        rows = pl.ds(*PIECE[piece])
        return remote(
            jb.at[k, rows], jb.at[lands, rows], f_send.at[k, n], j_recv.at[lands, piece], j_peer(to)
        )

    def j_line(k):
        dz = J_SLOTS[k][1]
        piece, lands, to = (0 if k in (1, 3) else 1), (5 if dz else 6), j_back(k)
        rows = pl.ds(*PIECE[piece])
        return remote(
            jb.at[k, rows], jb.at[lands, rows], f_send.at[k, 0], j_recv.at[lands, piece], j_peer(to)
        )

    def mix_copy(k):
        return remote(sbuf.at[k], mbuf.at[k - 3], r_send.at[k], m_recv.at[k - 3], i_peer(1))

    def r_copy(k):
        back = i_back(k)
        return remote(sbuf.at[k], fbuf.at[back], r_send.at[k], r_recv.at[back], i_peer(k))

    pl.semaphore_wait(barrier, len(LINE_I) + len(LINE_J))
    for k in NEAR_J:
        j_copy(k, 0).start()
    for k in LINE_I[:3]:
        i_copy(k).start()
    for k in NEAR_J:
        j_copy(k, 1).start()
    for k in LINE_I[3:]:
        i_copy(k).start()
    oacc[...] = jnp.zeros_like(oacc)

    def spread(k):
        packed = jb[k, pl.ds(TILE, PACK), :].astype(F32)
        for b in range(ROWS // PACK):
            jsq[k, pl.ds(b * PACK, PACK), :] = jnp.where(group == b, packed, 0.0).astype(BF16)

    spread(0)

    def fill(k):
        two = it[k, pl.ds(FEAT, 16), :]
        for r in range(FEAT + 16, TILE, 16):
            it[k, pl.ds(r, 16), :] = two

    fill(0)

    def want_i(k):
        if k in LINE_I:
            i_copy(i_back(k)).wait_recv()
            if k != 1:
                i_pass(k).start()
        else:
            i_pass(k - 3).wait_recv()
        fill(k)

    def want_j(k, piece):
        j_copy(j_back(k), piece).wait_recv()
        if piece == 0:
            spread(k)
        dy, dz = J_SLOTS[k]
        if k in NEAR_J and piece == (0 if k in (1, 3) else 1):
            j_line(k).start()
        if k in LINE_J and piece == (0 if dz else 1):
            for n in (1, 3):
                j_pass(k, n).start()

    def pass_far(k):
        j_pass(k, 2).start()

    events = {}

    def at(u, *what):
        events.setdefault(u, []).append(what)

    for k in range(1, N_I):
        at((FIRST_I[k] - 1) // BODY, want_i, k)
    for k in range(1, N_J):
        passed = 0 if J_SLOTS[k][1] else 1
        use = (FIRST_J[k] - 1) // BODY
        if k in LINE_J:
            at(min(use, 0 if k < 5 else FAR), want_j, k, passed)
            at(use, want_j, k, 1 - passed)
            at(3 if k in NEAR_J else FAR + 2, pass_far, k)
        else:
            at(use, want_j, k, 0)
            at(use, want_j, k, 1)

    def give(k):
        if k > 4:
            sbuf[k] = oacc[k].astype(BF16)
            mix_copy(k).start()
            return
        if k > 1:
            mix_copy(k + 3).wait_recv()
            sbuf[k] = (oacc[k] + mbuf[k].astype(F32)).astype(BF16)
        else:
            sbuf[k] = oacc[k].astype(BF16)
        r_copy(k).start()

    def work(e00, e01, e10, e11, o00, o01, o10, o11):
        e_acc = ((e00, e01), (e10, e11))
        o_acc = ((o00, o01), (o10, o11))
        ceiling = jnp.log(jnp.full((8, TILE), amplitude[0, 0], F32))[0:1]

        def inner(ik, jp, t):
            for q in range(2):
                pltpu.matmul_push_rhs(it[ik, :, pl.ds(q * TILE, TILE)], 0, q)
            slot, side = 2 * jp + t // 2, t % 2
            rows = jb[slot, pl.ds(HALF[side], TILE), :]
            lhs = jnp.concatenate([rows, jsq[slot, pl.ds(side * TILE, TILE), :]], axis=1)
            for q in range(2):
                pltpu.matmul_acc_lhs(e_acc[q][t % 2], lhs, load_staged_rhs=0)

        def expo(t):
            for q in range(2):
                e = pltpu.matmul_pop(e_acc[q][t % 2])
                kbuf[t % 2, q] = jnp.exp(jnp.minimum(e, ceiling)).astype(BF16)

        def product(jp, t, turn):
            slot, base = 2 * jp + t // 2, DIRS[t % 2]
            lhs = jnp.concatenate([jb[slot, pl.ds(base, COLS), :], jb[slot, pl.ds(base + COLS, COLS), :]], axis=1)
            for q in range(2):
                pltpu.matmul_push_rhs(kbuf[t % 2, q], 1, q)
            for q in range(2):
                pltpu.matmul_acc_lhs(o_acc[q][turn], lhs, load_staged_rhs=1)

        def collect(ik, turn):
            for q in range(2):
                oacc[ik, :, pl.ds(q * TILE, TILE)] += pltpu.matmul_pop(o_acc[q][turn])

        for what in events.pop(-1, []):
            what[0](*what[1:])
        inner(0, 0, 0)
        inner(0, 0, 1)
        expo(0)

        @pl.loop(0, UNITS // BODY)
        def _(b):
            @pl.when(marked(b, events))
            def _():
                for when, actions in sorted(events.items()):

                    @pl.when(b == when)
                    def _(actions=actions):
                        for what in actions:
                            what[0](*what[1:])

            for n in range(BODY):
                u = b * BODY + n
                ik, jp = where_is(u)
                ik_next, jp_next = where_is(jnp.minimum(u + 1, UNITS - 1))
                inner(ik, jp, 2)
                expo(1)
                product(jp, 0, n % 2)
                inner(ik, jp, 3)
                expo(2)
                collect(where_is(jnp.maximum(u - 1, 0))[0], 1 - n % 2)
                product(jp, 1, n % 2)
                inner(ik_next, jp_next, 0)
                expo(3)
                product(jp, 2, n % 2)
                inner(ik_next, jp_next, 1)
                expo(0)
                product(jp, 3, n % 2)

            @pl.when(b >= PHASE // BODY)
            def _():
                collect(where_is(b * BODY + BODY - 1)[0], (BODY - 1) % 2)
                for k in range(N_I - 1, 0, -1):
                    pl.when(b == DONE_I[k] // BODY)(functools.partial(give, k))

        for q in range(2):
            spare = pltpu.matmul_pop(e_acc[q][1])
            stat[1, 0] = spare[0:8, 0:FEAT]

    pl.run_scoped(
        work,
        *[pltpu.ACC(q)((TILE, TILE), F32) for q in (0, 0, 1, 1)],
        *[pltpu.ACC(q)((COLS, TILE), F32) for q in (0, 0, 1, 1)],
    )

    for copy in fetch[3:]:
        copy.wait()
    d = dirn[...]
    r = res[...]
    image = noise[...] * d + oacc[0]
    own = jnp.sum(r * r, axis=1, keepdims=True)
    for k in LINE_I:
        r_copy(i_back(k)).wait_recv()
        image = image + fbuf[k].astype(F32)
    lane = lax.broadcasted_iota(jnp.int32, (COLS, FEAT), 1)
    sums = jnp.zeros((COLS, FEAT), F32)
    sums = jnp.where(lane == 0, own, sums)
    for n, v in enumerate((d * image, r * image, image * image), 1):
        sums = jnp.where(lane == n, jnp.sum(v, axis=1, keepdims=True), sums)
    sums = jnp.transpose(jnp.concatenate([sums, jnp.zeros((FEAT - COLS, FEAT), F32)], axis=0))
    stat[0, 0] = sums[0:8]

    def a_copy(k):
        back = j_back(k)
        return remote(stat.at[0, 0], stat.at[0, back], a_send.at[k], a_recv.at[back], j_peer(k))

    def b_copy(k):
        back = i_back(k)
        return remote(stat.at[1, 0], stat.at[1, back], b_send.at[k], b_recv.at[back], i_peer(k))

    for k in range(1, N_J):
        a_copy(k).start()
    for k in LINE_I:
        i_copy(k).wait_send()
    for k in (2, 3, 4):
        i_pass(k).wait_send()
    for k in LINE_J:
        if k in NEAR_J:
            for piece in range(2):
                j_copy(k, piece).wait_send()
            j_line(k).wait_send()
        for n in (1, 3, 2):
            j_pass(k, n).wait_send()
    for k in range(1, N_I):
        (mix_copy if k > 4 else r_copy)(k).wait_send()
    for k in range(1, N_J):
        a_copy(j_back(k)).wait_recv()
    stat[1, 0] = jnp.sum(stat[0], axis=0)
    for k in range(1, N_I):
        b_copy(k).start()
    for k in range(1, N_J):
        a_copy(k).wait_send()
    for k in range(1, N_I):
        b_copy(i_back(k)).wait_recv()
    total = jnp.sum(stat[1, pl.ds(0, N_I)], axis=0)
    total = jnp.transpose(jnp.concatenate([total, jnp.zeros((FEAT - 8, FEAT), F32)], axis=0))
    old_norm, curvature, cross, square = [total[:COLS, n : n + 1] for n in range(4)]
    step = old_norm / curvature
    new_norm = jnp.maximum(old_norm - 2.0 * step * cross + step * step * square, 0.0)
    r_new = r - step * image
    out[0] = sol[...] + step * d
    out[1] = r_new
    out[2] = r_new + (new_norm / old_norm) * d

    for k in range(1, N_I):
        b_copy(k).wait_send()


def per_device(points, inv_length, amplitude, noise, sol, res, dirn):
    vmem = pl.BlockSpec(memory_space=pltpu.VMEM)
    hbm = pl.BlockSpec(memory_space=pltpu.HBM)
    out = jax.ShapeDtypeStruct((3, COLS, ROWS), F32)
    dma = pltpu.SemaphoreType.DMA
    outs = pl.pallas_call(
        kernel,
        out_shape=out,
        in_specs=[hbm, hbm, pl.BlockSpec(memory_space=pltpu.SMEM), hbm, hbm, hbm, hbm],
        out_specs=vmem,
        scratch_shapes=[
            pltpu.VMEM((ROWS, FEAT), BF16),
            pltpu.VMEM((1, FEAT), F32),
            pltpu.VMEM((1, ROWS), F32),
            pltpu.VMEM((COLS, ROWS), F32),
            pltpu.VMEM((COLS, ROWS), F32),
            pltpu.VMEM((COLS, ROWS), F32),
            pltpu.VMEM((N_I, TILE, ROWS), BF16),
            pltpu.VMEM((N_J, SHIP, FEAT), BF16),
            pltpu.VMEM((N_J, ROWS, FEAT), BF16),
            pltpu.VMEM((N_I, COLS, ROWS), F32),
            pltpu.VMEM((2, 2, TILE, TILE), BF16),
            pltpu.VMEM((N_I, COLS, ROWS), BF16),
            pltpu.VMEM((5, COLS, ROWS), BF16),
            pltpu.VMEM((5, COLS, ROWS), BF16),
            pltpu.VMEM((2, N_J, 8, FEAT), F32),
            dma((6,)),
            dma((N_I,)),
            dma((N_I,)),
            dma((N_J, 2)),
            dma((N_J, 2)),
            dma((7, 4)),
            dma((5,)),
            dma((N_I,)),
            dma((5,)),
            dma((N_J,)),
            dma((N_J,)),
            dma((N_I,)),
            dma((N_I,)),
        ],
        compiler_params=pltpu.CompilerParams(
            collective_id=0, has_side_effects=True, vmem_limit_bytes=64 * 1024 * 1024
        ),
        name="cg_step",
    )(points, inv_length.reshape(1, -1), amplitude.reshape(1, 1), noise.reshape(1, -1), sol.T, res.T, dirn.T)
    return outs[0].T, outs[1].T, outs[2].T


def solution(mesh):
    placed = (
        P(("blk", "split"), None),
        P(),
        P(),
        P(("blk", "split")),
        P(("blk", "split"), None),
        P(("blk", "split"), None),
        P(("blk", "split"), None),
    )

    def whole(*args):
        with jax.sharding.use_abstract_mesh(mesh.abstract_mesh):
            return jax.shard_map(
                per_device,
                mesh=mesh,
                in_specs=placed,
                out_specs=(P(("blk", "split"), None),) * 3,
                check_vma=False,
            )(*args)

    return whole
```
